1024 devices in a mesh: row: 32 (over y, x), col: 4 (over z_hi, core), depth: 8 (over z_lo).
Axes of the slice: x: 4, y: 8, z: 16 (z_hi: 2, z_lo: 8; z = z_hi * 8 + z_lo), core: 2. Of those that a mesh axis runs over, the one named last changes fastest.
Arguments:
- blocks: float32 [1024, 10, 128, 128], P(('row', 'col', 'depth')), may hold values from -1.5 to 1.5
- columns: int32 [1024, 10], replicated, may hold values from 0 to 1023, as said below
Outputs:
- product: float32 [1024, 10, 128, 128], P(('row', 'col', 'depth'))
The draws below stay inside these ranges and needn't reach their ends.
Inputs may be any that keep to these rules, and one draw needn't show every extreme that they name: The columns of a block row are distinct. Slot s of block row i holds block column (i + t) mod 1024 with t ≡ s − i (mod 8) and -16 < t < 16; slot i mod 8 holds column i itself.
All inputs are finite; a program needn't handle non-finite values.
Results may differ from the reference program's by a relative error of at most 0.0003.
Values sent between devices are 32-bit elements; how exact they have to be, the bound alone decides.
No kernel may reach another device: no remote copies, remote signals or barrier semaphores. Data moves between devices by JAX's collectives and lax.ppermute only.
A program may use at most 64 MiB of HBM per device.

```python
import jax
import jax.numpy as jnp
from jax import lax

BLOCK = 128
SLOTS = 10
NBR = 1024
N_DEPTH = 8


def draw_columns(key, part):
    key = jax.random.fold_in(key, 7)
    row_ids = jnp.arange(NBR, dtype=jnp.int32)[:, None]
    slot_ids = jnp.arange(SLOTS, dtype=jnp.int32)[None, :]
    residue = (slot_ids - row_ids) % N_DEPTH
    pick_one = jax.random.randint(key, (NBR, SLOTS), 0, 2, dtype=jnp.int32)
    positive = (residue > 0).astype(jnp.int32)
    first_kind = residue - N_DEPTH * pick_one * positive
    second_kind = positive * (residue + N_DEPTH - 3 * N_DEPTH * pick_one) + (1 - positive) * (N_DEPTH - 2 * N_DEPTH * pick_one)
    is_first = (slot_ids < N_DEPTH).astype(jnp.int32)
    shift_by = is_first * first_kind + (1 - is_first) * second_kind
    return ((row_ids + shift_by) % NBR).astype(jnp.int32)


def levels(own_key, extent, cuts, least, largest):
    loudness, own = 1.0, jax.random.fold_in(own_key, 6)
    for axis_at, parts in cuts:
        heights = jnp.exp(jax.random.uniform(jax.random.fold_in(own, axis_at), (parts,), jnp.float32, least / len(cuts), largest / len(cuts)))
        loudness = loudness * jnp.repeat(heights, extent[axis_at] // parts).reshape([-1 if axis == axis_at else 1 for axis in range(len(extent))])
    return loudness


def noise(key, dims, width, bound, split=(), kind=jnp.bfloat16):
    level = levels(key, dims, split, -0.22, 0.18) if split else 1.0
    array = jax.random.normal(key, dims, jnp.float32) * width * level
    return jnp.minimum(jnp.maximum(array, -bound), bound).astype(kind)


def setup_inputs(seed: int = 0) -> dict:
    seeds = jax.random.split(jax.random.key(seed), 3)
    blocks = noise(seeds[0], (NBR, SLOTS, BLOCK, BLOCK), 0.25, 1.5, ((0, 1024),), jnp.float32)
    columns = draw_columns(jax.random.fold_in(seeds[2], 71), 0)
    return {"blocks": blocks, "columns": columns}


def reference(blocks, columns):
    def one_row(row_index):
        row_cols = columns[row_index]
        operand = blocks[row_index]
        partner = jnp.take(blocks, row_cols, axis=0)
        partner_cols = jnp.take(columns, row_cols, axis=0)
        matched = (partner_cols[:, :, None] == row_cols[None, None, :]).astype(jnp.float32)
        chosen = jnp.einsum("sro,srbc->sobc", matched, partner, precision=lax.Precision.HIGHEST)
        return jnp.einsum("sab,sobc->oac", operand, chosen, precision=lax.Precision.HIGHEST)

    return lax.map(one_row, jnp.arange(NBR, dtype=jnp.int32))
```

```python
import functools

import jax
import jax.numpy as jnp
from jax import lax
from jax.experimental import pallas as pl
from jax.experimental.pallas import tpu as pltpu
from jax.sharding import PartitionSpec as P


def ring_pairs(depth, chips, steps):
    pairs = []
    for chip in chips:
        for core in range(2):
            to = (chip + (steps if core == 0 else -steps)) % (2 * depth)
            pairs.append(
                (
                    (chip // depth * 2 + core) * depth + chip % depth,
                    (to // depth * 2 + core) * depth + to % depth,
                )
            )
    return pairs


def flip_pairs(depth):
    return [(n, n ^ depth) for n in range(4 * depth)]


def ghost_pairs(lines, depth, flip):
    pairs = []
    for line in range(lines):
        for n in range(4 * depth):
            other = (line - 1 if n < 2 * depth else line + 1) % lines
            pairs.append((line * 4 * depth + n, other * 4 * depth + (n ^ depth if flip else n)))
    return pairs


def split(value):
    high = value.astype(jnp.bfloat16)
    return high, (value - high.astype(jnp.float32)).astype(jnp.bfloat16)


def step_kernel(depth, slots, step, rows, targets, fresh, info, *refs):
    held, refs = refs[: len(rows)], refs[len(rows) :]
    factors, refs = refs[: len(targets)], refs[len(targets) :]
    if not fresh:
        refs = refs[len(targets) :]
    sums, refs = refs[: len(targets)], refs[len(targets) :]
    row_buf, factor_buf, sum_buf, row_sem, factor_sem, sum_sem = refs

    place, core = info[0], info[1]
    half, low = place // depth, place % depth
    there = (place + 2 * depth - step + 2 * step * core) % (2 * depth)
    cls = there % depth
    line_rows = 4 * depth

    def column(row, slot):
        return info[2 + row * slots + slot]

    def held_row(which):
        q = core + which * (1 - 2 * core)
        return line_rows + 2 * depth * (there // depth) + depth * q + cls

    def target_row(which):
        q = core + (which % 2) * (1 - 2 * core)
        mine = line_rows + 2 * depth * half + depth * q + low
        return mine + (line_rows - 2 * line_rows * half if which >= 2 else 0)

    def find(k, i):
        more = jnp.minimum(cls + depth, slots - 1)
        first = column(i, cls) == k
        second = jnp.logical_and(cls + depth < slots, column(i, more) == k)
        return jnp.logical_or(first, second), jnp.where(first, cls, more)

    k_of = [held_row(r) for r in rows]
    i_of = [target_row(t) for t in targets]
    found = [[find(k, i) for i in i_of] for k in k_of]
    row_used = [functools.reduce(jnp.logical_or, [f[0] for f in per]) for per in found]
    sum_used = [
        functools.reduce(jnp.logical_or, [found[r][t][0] for r in range(len(rows))])
        for t in range(len(targets))
    ]

    def row_copy(r):
        return pltpu.make_async_copy(held[r], row_buf.at[r], row_sem.at[r])

    def factor_copy(r, t):
        n = r * len(targets) + t
        return pltpu.make_async_copy(
            factors[t].at[found[r][t][1]], factor_buf.at[n], factor_sem.at[n]
        )

    def sum_load(t):
        return pltpu.make_async_copy(sums[t], sum_buf.at[t], sum_sem.at[t])

    def sum_store(t):
        return pltpu.make_async_copy(sum_buf.at[t], sums[t], sum_sem.at[t])

    for phase in ("start", "wait"):
        for r in range(len(rows)):
            pl.when(row_used[r])(getattr(row_copy(r), phase))
            for t in range(len(targets)):
                pl.when(found[r][t][0])(getattr(factor_copy(r, t), phase))
        if not fresh:
            for t in range(len(targets)):
                pl.when(sum_used[t])(getattr(sum_load(t), phase))
        elif phase == "start":
            for t in range(len(targets)):
                sum_buf[t] = jnp.zeros(sum_buf.shape[1:], jnp.float32)

    def select(options, n):
        out = options[0]
        for m in range(1, len(options)):
            out = jnp.where(n == m, options[m], out)
        return out

    def product(n, carry):
        r, t = n // len(targets), n % len(targets)
        k, i = select(k_of, r), select(i_of, t)

        @pl.when(find(k, i)[0])
        def _():
            a_high, a_low = split(factor_buf[n])
            for pair in range(0, slots, 2):
                blocks = []
                for o in (pair, pair + 1):
                    goal = column(i, o)
                    match, where = column(k, o) == goal, o
                    twin = o + depth if o + depth < slots else o - depth
                    if twin >= 0:
                        second = column(k, twin) == goal
                        match, where = jnp.logical_or(match, second), jnp.where(second, twin, o)
                    block = row_buf[r, where]
                    blocks.append(jnp.where(match, block, jnp.zeros_like(block)))
                b_high, b_low = split(jnp.concatenate(blocks, axis=1))
                dot = functools.partial(jnp.dot, preferred_element_type=jnp.float32)
                part = dot(a_high, b_high) + (dot(a_high, b_low) + dot(a_low, b_high))
                edge = part.shape[0]
                sum_buf[t, pair] += part[:, :edge]
                sum_buf[t, pair + 1] += part[:, edge:]

        return carry

    lax.fori_loop(0, len(rows) * len(targets), product, 0)

    for phase in ("start", "wait"):
        for t in range(len(targets)):
            if fresh:
                getattr(sum_store(t), phase)()
            else:
                pl.when(sum_used[t])(getattr(sum_store(t), phase))


def step_call(depth, step, rows, targets, info, held, factors, sums=None):
    slots, edge = held[0].shape[:2]
    fresh = sums is None
    shape = jax.ShapeDtypeStruct(held[0].shape, jnp.float32)
    hbm = pl.BlockSpec(memory_space=pl.ANY)
    operands = [info, *held, *factors] + ([] if fresh else list(sums))
    first = 1 + len(held) + len(factors)
    count = len(rows) * len(targets)
    return pl.pallas_call(
        functools.partial(step_kernel, depth, slots, step, rows, targets, fresh),
        out_shape=[shape] * len(targets),
        in_specs=[pl.BlockSpec(memory_space=pltpu.SMEM)] + [hbm] * (len(operands) - 1),
        out_specs=[hbm] * len(targets),
        input_output_aliases={} if fresh else {first + t: t for t in range(len(targets))},
        scratch_shapes=[
            pltpu.VMEM((len(rows), *shape.shape), jnp.float32),
            pltpu.VMEM((count, edge, edge), jnp.float32),
            pltpu.VMEM((len(targets), *shape.shape), jnp.float32),
            pltpu.SemaphoreType.DMA((len(rows),)),
            pltpu.SemaphoreType.DMA((count,)),
            pltpu.SemaphoreType.DMA((len(targets),)),
        ],
        compiler_params=pltpu.CompilerParams(vmem_limit_bytes=24 << 20),
        cost_estimate=pl.CostEstimate(
            flops=200_000_000, bytes_accessed=8_000_000, transcendentals=0
        ),
        name="products",
    )(*operands)


def body(blocks, columns):
    depth = lax.axis_size("depth")
    lines = lax.axis_size("row")
    block_rows, slots = columns.shape
    line_rows = 4 * depth
    ring, every = ("col", "depth"), ("row", "col", "depth")
    col = lax.axis_index("col")
    place = (col // 2) * depth + lax.axis_index("depth")
    base = (lax.axis_index("row") - 1) * line_rows + block_rows
    near = jnp.take(columns, (base + jnp.arange(3 * line_rows)) % block_rows, axis=0)
    near = (near - base + 2 * block_rows) % block_rows
    info = jnp.concatenate(
        [jnp.stack([place, col % 2]).astype(jnp.int32), near.reshape(-1)]
    )

    own = blocks[0]
    chips = range(2 * depth)
    onward = ring_pairs(depth, chips, 1)
    last = [p for p in onward if p[1] % depth < slots - depth]
    homeward = [(b, a) for a, b in ghost_pairs(lines, depth, False)]
    homeward_flip = [(b, a) for a, b in ghost_pairs(lines, depth, True)]

    held = [own, lax.ppermute(own, ring, flip_pairs(depth))]
    ghost = lax.ppermute(own, every, ghost_pairs(lines, depth, False))
    ghost_flip = lax.ppermute(own, every, ghost_pairs(lines, depth, True))
    factors = [held[0], held[1], ghost, ghost_flip]
    (mine,) = step_call(depth, 0, (0, 1), (0,), info, held, factors[:1])
    sums = [mine] + [jnp.zeros_like(own) for _ in range(3)]
    held = [lax.ppermute(h, ring, onward) for h in held]
    for step in range(1, depth):
        held[0], sums = lax.optimization_barrier((held[0], sums))
        if step < depth - 1:
            after = [lax.ppermute(h, ring, onward) for h in held]
        else:
            after = [lax.ppermute(held[1], ring, last)]
        sums = list(step_call(depth, step, (0, 1), (0, 1, 2, 3), info, held, factors, sums))
        held = after
    sums[0], sums[2] = step_call(
        depth, depth, (1,), (0, 2), info, held, [factors[0], factors[2]], [sums[0], sums[2]]
    )
    total = sums[0] + lax.ppermute(sums[1], ring, flip_pairs(depth))
    total = total + lax.ppermute(sums[2], every, homeward)
    total = total + lax.ppermute(sums[3], every, homeward_flip)
    return total[None]


def solution(mesh):
    placed = (P(("row", "col", "depth"), None, None, None), P())
    return jax.shard_map(
        body,
        mesh=mesh,
        in_specs=placed,
        out_specs=P(("row", "col", "depth"), None, None, None),
        check_vma=False,
    )
```

```python
import functools

import jax
import jax.numpy as jnp
from jax import lax
from jax.experimental import pallas as pl
from jax.experimental.pallas import tpu as pltpu
from jax.sharding import PartitionSpec as P


def device(line, place, core, depth):
    return ((line * 2 + place // depth) * 2 + core) * depth + place % depth


def hop_pairs(lines, depth, step, which, across=False):
    pairs = []
    for line in range(lines):
        for place in range(2 * depth):
            for core in range(2):
                way = 1 - 2 * core
                origin = (place - way * (step - 1)) % (2 * depth)
                to = (place + way) % (2 * depth)
                crosses = place // depth - to // depth if origin // depth == core ^ which else 0
                pairs.append(
                    (
                        device(line, place, core, depth),
                        device((line + crosses) % lines, to, core ^ across, depth),
                    )
                )
    return pairs


def flip_pairs(depth):
    return [(n, n ^ depth) for n in range(4 * depth)]


def line_pairs(lines, depth):
    return [
        (device(line, place, core, depth), device((line - 1 + 2 * core) % lines, place, core, depth))
        for line in range(lines)
        for place in range(2 * depth)
        for core in range(2)
    ]


def split(value):
    high = value.astype(jnp.bfloat16)
    return high, (value - high.astype(jnp.float32)).astype(jnp.bfloat16)


def step_kernel(depth, slots, step, rows, targets, pairs, fresh, info, *refs):
    held, refs = refs[: len(rows)], refs[len(rows) :]
    factors, refs = refs[: len(targets)], refs[len(targets) :]
    if not fresh:
        refs = refs[len(targets) :]
    sums, refs = refs[: len(targets)], refs[len(targets) :]
    row_buf, factor_buf, sum_buf, row_sem, factor_sem, sum_sem = refs

    place, core = info[0], info[1]
    half, low = place // depth, place % depth
    there = (place + 2 * depth - step + 2 * step * core) % (2 * depth)
    origin, cls = there // depth, there % depth
    line_rows = 4 * depth

    def column(row, slot):
        return info[2 + row * slots + slot]

    def held_row(which):
        q = core + which * (1 - 2 * core)
        line = 1 + jnp.where(origin == q, half - origin, 0)
        return line_rows * line + 2 * depth * origin + depth * q + cls

    def target_row(which):
        q = core + (which == 1) * (1 - 2 * core)
        line = 1 + (which == 2) * (1 - 2 * core)
        return line_rows * line + 2 * depth * half + depth * q + low

    def find(k, i):
        more = jnp.minimum(cls + depth, slots - 1)
        first = column(i, cls) == k
        second = jnp.logical_and(cls + depth < slots, column(i, more) == k)
        return jnp.logical_or(first, second), jnp.where(first, cls, more)

    k_of = [held_row(r) for r in rows]
    i_of = [target_row(t) for t in targets]
    found = [find(k_of[r], i_of[t]) for r, t in pairs]

    def any_of(where):
        return functools.reduce(jnp.logical_or, [f[0] for f, p in zip(found, pairs) if where(p)])

    row_used = [any_of(lambda p, r=r: p[0] == r) for r in range(len(rows))]
    sum_used = [any_of(lambda p, t=t: p[1] == t) for t in range(len(targets))]

    def row_copy(r):
        return pltpu.make_async_copy(held[r], row_buf.at[r], row_sem.at[r])

    def factor_copy(n):
        t = pairs[n][1]
        return pltpu.make_async_copy(
            factors[t].at[found[n][1]], factor_buf.at[n], factor_sem.at[n]
        )

    def sum_load(t):
        return pltpu.make_async_copy(sums[t], sum_buf.at[t], sum_sem.at[t])

    def sum_store(t):
        return pltpu.make_async_copy(sum_buf.at[t], sums[t], sum_sem.at[t])

    for phase in ("start", "wait"):
        for r in range(len(rows)):
            pl.when(row_used[r])(getattr(row_copy(r), phase))
        for n in range(len(pairs)):
            pl.when(found[n][0])(getattr(factor_copy(n), phase))
        if not fresh:
            for t in range(len(targets)):
                pl.when(sum_used[t])(getattr(sum_load(t), phase))
        elif phase == "start":
            for t in range(len(targets)):
                sum_buf[t] = jnp.zeros(sum_buf.shape[1:], jnp.float32)

    def select(options, n):
        out = options[0]
        for m in range(1, len(options)):
            out = jnp.where(n == m, options[m], out)
        return out

    def product(n, carry):
        r = select([p[0] for p in pairs], n)
        t = select([p[1] for p in pairs], n)
        k, i = select(k_of, r), select(i_of, t)

        @pl.when(find(k, i)[0])
        def _():
            a_high, a_low = split(factor_buf[n])
            for pair in range(0, slots, 2):
                blocks = []
                for o in (pair, pair + 1):
                    goal = column(i, o)
                    match, where = column(k, o) == goal, o
                    twin = o + depth if o + depth < slots else o - depth
                    if twin >= 0:
                        second = column(k, twin) == goal
                        match, where = jnp.logical_or(match, second), jnp.where(second, twin, o)
                    block = row_buf[r, where]
                    blocks.append(jnp.where(match, block, jnp.zeros_like(block)))
                b_high, b_low = split(jnp.concatenate(blocks, axis=1))
                dot = functools.partial(jnp.dot, preferred_element_type=jnp.float32)
                part = dot(a_high, b_high) + (dot(a_high, b_low) + dot(a_low, b_high))
                edge = part.shape[0]
                sum_buf[t, pair] += part[:, :edge]
                sum_buf[t, pair + 1] += part[:, edge:]

        return carry

    lax.fori_loop(0, len(pairs), product, 0)

    for phase in ("start", "wait"):
        for t in range(len(targets)):
            if fresh:
                getattr(sum_store(t), phase)()
            else:
                pl.when(sum_used[t])(getattr(sum_store(t), phase))


def step_call(depth, step, rows, targets, pairs, info, held, factors, sums=None):
    slots, edge = held[0].shape[:2]
    fresh = sums is None
    shape = jax.ShapeDtypeStruct(held[0].shape, jnp.float32)
    hbm = pl.BlockSpec(memory_space=pl.ANY)
    operands = [info, *held, *factors] + ([] if fresh else list(sums))
    first = 1 + len(held) + len(factors)
    return list(
        pl.pallas_call(
            functools.partial(step_kernel, depth, slots, step, rows, targets, pairs, fresh),
            out_shape=[shape] * len(targets),
            in_specs=[pl.BlockSpec(memory_space=pltpu.SMEM)] + [hbm] * (len(operands) - 1),
            out_specs=[hbm] * len(targets),
            input_output_aliases={} if fresh else {first + t: t for t in range(len(targets))},
            scratch_shapes=[
                pltpu.VMEM((len(rows), *shape.shape), jnp.float32),
                pltpu.VMEM((len(pairs), edge, edge), jnp.float32),
                pltpu.VMEM((len(targets), *shape.shape), jnp.float32),
                pltpu.SemaphoreType.DMA((len(rows),)),
                pltpu.SemaphoreType.DMA((len(pairs),)),
                pltpu.SemaphoreType.DMA((len(targets),)),
            ],
            compiler_params=pltpu.CompilerParams(vmem_limit_bytes=24 << 20),
            cost_estimate=pl.CostEstimate(
                flops=200_000_000, bytes_accessed=8_000_000, transcendentals=0
            ),
            name="products",
        )(*operands)
    )


def body(blocks, columns):
    depth = lax.axis_size("depth")
    lines = lax.axis_size("row")
    block_rows, slots = columns.shape
    line_rows = 4 * depth
    ring, every = ("col", "depth"), ("row", "col", "depth")
    col = lax.axis_index("col")
    place = (col // 2) * depth + lax.axis_index("depth")
    base = (lax.axis_index("row") - 1) * line_rows + block_rows
    near = jnp.take(columns, (base + jnp.arange(3 * line_rows)) % block_rows, axis=0)
    near = (near - base + 2 * block_rows) % block_rows
    info = jnp.concatenate(
        [jnp.stack([place, col % 2]).astype(jnp.int32), near.reshape(-1)]
    )

    def hop(held, step, which):
        return lax.ppermute(held[which], every, hop_pairs(lines, depth, step, which))

    def flip(value):
        return lax.ppermute(value, ring, flip_pairs(depth))

    own = blocks[0]
    held = [own, flip(own)]
    away = line_pairs(lines, depth)
    ghost = lax.ppermute(own, every, away)
    factors = [held[0], held[1], ghost]
    sums = step_call(depth, 0, (0, 1), (0,), ((0, 0), (1, 0)), info, held, factors[:1])
    sums += [jnp.zeros_like(own) for _ in range(2)]
    held = [hop(held, 1, which) for which in range(2)]
    for step in range(1, depth - 1):
        held[0], sums = lax.optimization_barrier((held[0], sums))
        after = [hop(held, step + 1, which) for which in range(2)]
        pairs = ((0, 0), (0, 1), (0, 2), (1, 0), (1, 1))
        sums = step_call(depth, step, (0, 1), (0, 1, 2), pairs, info, held, factors, sums)
        held = after
    last = depth - 1
    held[0], sums = lax.optimization_barrier((held[0], sums))
    far = [
        p for p in hop_pairs(lines, depth, depth, 0, across=True) if p[1] % depth < slots - depth
    ]
    far = lax.ppermute(held[0], every, far)
    (foreign,) = step_call(
        depth, last, (0,), (2,), ((0, 0),), info, held[:1], factors[2:], sums[2:]
    )
    foreign = lax.ppermute(foreign, every, [(b, a) for a, b in away])
    mine, other = step_call(
        depth, last, (0, 1), (0, 1), ((0, 0), (0, 1), (1, 0), (1, 1)), info, held, factors[:2], sums[:2]
    )
    other = flip(other)
    (mine,) = step_call(depth, depth, (1,), (0,), ((0, 0),), info, [far], factors[:1], [mine])
    return (mine + other + foreign)[None]


def solution(mesh):
    placed = (P(("row", "col", "depth"), None, None, None), P())
    return jax.shard_map(
        body,
        mesh=mesh,
        in_specs=placed,
        out_specs=P(("row", "col", "depth"), None, None, None),
        check_vma=False,
    )
```

```python
import functools

import jax
import jax.numpy as jnp
from jax import lax
from jax.experimental import pallas as pl
from jax.experimental.pallas import tpu as pltpu
from jax.sharding import PartitionSpec as P


def device(line, place, core, depth):
    return ((line * 2 + place // depth) * 2 + core) * depth + place % depth


def hop_pairs(lines, depth, step, which, across=False):
    pairs = []
    for line in range(lines):
        for place in range(2 * depth):
            for core in range(2):
                way = 1 - 2 * core
                origin = (place - way * (step - 1)) % (2 * depth)
                to = (place + way) % (2 * depth)
                crosses = place // depth - to // depth if origin // depth == core ^ which else 0
                pairs.append(
                    (
                        device(line, place, core, depth),
                        device((line + crosses) % lines, to, core ^ across, depth),
                    )
                )
    return pairs


def flip_pairs(depth):
    return [(n, n ^ depth) for n in range(4 * depth)]


def line_pairs(lines, depth):
    return [
        (device(line, place, core, depth), device((line - 1 + 2 * core) % lines, place, core, depth))
        for line in range(lines)
        for place in range(2 * depth)
        for core in range(2)
    ]


def split(value):
    high = value.astype(jnp.bfloat16)
    return high, (value - high.astype(jnp.float32)).astype(jnp.bfloat16)


def step_kernel(depth, slots, step, rows, targets, pairs, fresh, info, *refs):
    held, refs = refs[: len(rows)], refs[len(rows) :]
    factors, refs = refs[: len(targets)], refs[len(targets) :]
    if not fresh:
        refs = refs[len(targets) :]
    sums, refs = refs[: len(targets)], refs[len(targets) :]
    row_buf, factor_buf, sum_buf, row_sem, factor_sem, sum_sem = refs

    place, core = info[0], info[1]
    half, low = place // depth, place % depth
    there = (place + 2 * depth - step + 2 * step * core) % (2 * depth)
    origin, cls = there // depth, there % depth
    line_rows = 4 * depth

    def column(row, slot):
        return info[2 + row * slots + slot]

    def held_row(which):
        q = core + which * (1 - 2 * core)
        line = 1 + jnp.where(origin == q, half - origin, 0)
        return line_rows * line + 2 * depth * origin + depth * q + cls

    def target_row(which):
        q = core + (which == 1) * (1 - 2 * core)
        line = 1 + (which == 2) * (1 - 2 * core)
        return line_rows * line + 2 * depth * half + depth * q + low

    def find(k, i):
        more = jnp.minimum(cls + depth, slots - 1)
        first = column(i, cls) == k
        second = jnp.logical_and(cls + depth < slots, column(i, more) == k)
        return jnp.logical_or(first, second), jnp.where(first, cls, more)

    k_of = [held_row(r) for r in rows]
    i_of = [target_row(t) for t in targets]
    found = [find(k_of[r], i_of[t]) for r, t in pairs]

    def any_of(where):
        return functools.reduce(jnp.logical_or, [f[0] for f, p in zip(found, pairs) if where(p)])

    row_used = [any_of(lambda p, r=r: p[0] == r) for r in range(len(rows))]
    sum_used = [any_of(lambda p, t=t: p[1] == t) for t in range(len(targets))]

    def row_copy(r):
        return pltpu.make_async_copy(held[r], row_buf.at[r], row_sem.at[r])

    def factor_copy(n):
        t = pairs[n][1]
        return pltpu.make_async_copy(
            factors[t].at[found[n][1]], factor_buf.at[n], factor_sem.at[n]
        )

    def sum_load(t):
        return pltpu.make_async_copy(sums[t], sum_buf.at[t], sum_sem.at[t])

    def sum_store(t):
        return pltpu.make_async_copy(sum_buf.at[t], sums[t], sum_sem.at[t])

    for phase in ("start", "wait"):
        for r in range(len(rows)):
            pl.when(row_used[r])(getattr(row_copy(r), phase))
        for n in range(len(pairs)):
            pl.when(found[n][0])(getattr(factor_copy(n), phase))
        if not fresh:
            for t in range(len(targets)):
                pl.when(sum_used[t])(getattr(sum_load(t), phase))
        elif phase == "start":
            for t in range(len(targets)):
                sum_buf[t] = jnp.zeros(sum_buf.shape[1:], jnp.float32)

    def select(options, n):
        out = options[0]
        for m in range(1, len(options)):
            out = jnp.where(n == m, options[m], out)
        return out

    def product(n, carry):
        r = select([p[0] for p in pairs], n)
        t = select([p[1] for p in pairs], n)
        k, i = select(k_of, r), select(i_of, t)

        @pl.when(find(k, i)[0])
        def _():
            a_high, a_low = split(factor_buf[n])
            for pair in range(0, slots, 2):
                blocks = []
                for o in (pair, pair + 1):
                    goal = column(i, o)
                    match, where = column(k, o) == goal, o
                    twin = o + depth if o + depth < slots else o - depth
                    if twin >= 0:
                        second = column(k, twin) == goal
                        match, where = jnp.logical_or(match, second), jnp.where(second, twin, o)
                    block = row_buf[r, where]
                    blocks.append(jnp.where(match, block, jnp.zeros_like(block)))
                b_high, b_low = split(jnp.concatenate(blocks, axis=1))
                dot = functools.partial(jnp.dot, preferred_element_type=jnp.float32)
                part = dot(a_high, b_high) + (dot(a_high, b_low) + dot(a_low, b_high))
                edge = part.shape[0]
                sum_buf[t, pair] += part[:, :edge]
                sum_buf[t, pair + 1] += part[:, edge:]

        return carry

    lax.fori_loop(0, len(pairs), product, 0)

    for phase in ("start", "wait"):
        for t in range(len(targets)):
            if fresh:
                getattr(sum_store(t), phase)()
            else:
                pl.when(sum_used[t])(getattr(sum_store(t), phase))


def step_call(depth, step, rows, targets, pairs, info, held, factors, sums=None):
    slots, edge = held[0].shape[:2]
    fresh = sums is None
    shape = jax.ShapeDtypeStruct(held[0].shape, jnp.float32)
    hbm = pl.BlockSpec(memory_space=pl.ANY)
    operands = [info, *held, *factors] + ([] if fresh else list(sums))
    first = 1 + len(held) + len(factors)
    return list(
        pl.pallas_call(
            functools.partial(step_kernel, depth, slots, step, rows, targets, pairs, fresh),
            out_shape=[shape] * len(targets),
            in_specs=[pl.BlockSpec(memory_space=pltpu.SMEM)] + [hbm] * (len(operands) - 1),
            out_specs=[hbm] * len(targets),
            input_output_aliases={} if fresh else {first + t: t for t in range(len(targets))},
            scratch_shapes=[
                pltpu.VMEM((len(rows), *shape.shape), jnp.float32),
                pltpu.VMEM((len(pairs), edge, edge), jnp.float32),
                pltpu.VMEM((len(targets), *shape.shape), jnp.float32),
                pltpu.SemaphoreType.DMA((len(rows),)),
                pltpu.SemaphoreType.DMA((len(pairs),)),
                pltpu.SemaphoreType.DMA((len(targets),)),
            ],
            compiler_params=pltpu.CompilerParams(vmem_limit_bytes=24 << 20),
            cost_estimate=pl.CostEstimate(
                flops=200_000_000, bytes_accessed=8_000_000, transcendentals=0
            ),
            name="products",
        )(*operands)
    )


def body(blocks, columns):
    depth = lax.axis_size("depth")
    lines = lax.axis_size("row")
    block_rows, slots = columns.shape
    line_rows = 4 * depth
    ring, every = ("col", "depth"), ("row", "col", "depth")
    col = lax.axis_index("col")
    place = (col // 2) * depth + lax.axis_index("depth")
    base = (lax.axis_index("row") - 1) * line_rows + block_rows
    near = jnp.take(columns, (base + jnp.arange(3 * line_rows)) % block_rows, axis=0)
    near = (near - base + 2 * block_rows) % block_rows
    info = jnp.concatenate(
        [jnp.stack([place, col % 2]).astype(jnp.int32), near.reshape(-1)]
    )

    def hop(held, step, which):
        return lax.ppermute(held[which], every, hop_pairs(lines, depth, step, which))

    def flip(value):
        return lax.ppermute(value, ring, flip_pairs(depth))

    own = blocks[0]
    other, info = lax.optimization_barrier((flip(own), info))
    held = [own, other]
    away = line_pairs(lines, depth)
    ghost = lax.ppermute(own, every, away)
    factors = [held[0], held[1], ghost]
    sums = step_call(depth, 0, (0, 1), (0,), ((0, 0), (1, 0)), info, held, factors[:1])
    sums += [jnp.zeros_like(own) for _ in range(2)]
    held = [hop(held, 1, which) for which in range(2)]
    for step in range(1, depth - 1):
        held[0], sums = lax.optimization_barrier((held[0], sums))
        after = [hop(held, step + 1, which) for which in range(2)]
        pairs = ((0, 0), (0, 1), (0, 2), (1, 0), (1, 1))
        sums = step_call(depth, step, (0, 1), (0, 1, 2), pairs, info, held, factors, sums)
        held = after
    last = depth - 1
    held[0], sums = lax.optimization_barrier((held[0], sums))
    far = [
        p for p in hop_pairs(lines, depth, depth, 0, across=True) if p[1] % depth < slots - depth
    ]
    far = lax.ppermute(held[0], every, far)
    (foreign,) = step_call(
        depth, last, (0,), (2,), ((0, 0),), info, held[:1], factors[2:], sums[2:]
    )
    foreign = lax.ppermute(foreign, every, [(b, a) for a, b in away])
    mine, other = step_call(
        depth, last, (0, 1), (0, 1), ((0, 0), (0, 1), (1, 0), (1, 1)), info, held, factors[:2], sums[:2]
    )
    other = flip(other)
    (mine,) = step_call(depth, depth, (1,), (0,), ((0, 0),), info, [far], factors[:1], [mine])
    return (mine + other + foreign)[None]


def solution(mesh):
    placed = (P(("row", "col", "depth"), None, None, None), P())
    return jax.shard_map(
        body,
        mesh=mesh,
        in_specs=placed,
        out_specs=P(("row", "col", "depth"), None, None, None),
        check_vma=False,
    )
```

```python
import functools

import jax
import jax.numpy as jnp
from jax import lax
from jax.experimental import pallas as pl
from jax.experimental.pallas import tpu as pltpu
from jax.sharding import PartitionSpec as P


CUTS = ((5,), (5,))


def device(line, place, core, depth):
    return ((line * 2 + place // depth) * 2 + core) * depth + place % depth


def hop_pairs(lines, depth, step, which, across=False):
    pairs = []
    for line in range(lines):
        for place in range(2 * depth):
            for core in range(2):
                way = 1 - 2 * core
                origin = (place - way * (step - 1)) % (2 * depth)
                to = (place + way) % (2 * depth)
                crosses = place // depth - to // depth if origin // depth == core ^ which else 0
                pairs.append(
                    (
                        device(line, place, core, depth),
                        device((line + crosses) % lines, to, core ^ across, depth),
                    )
                )
    return pairs


def flip_pairs(depth):
    return [(n, n ^ depth) for n in range(4 * depth)]


def line_pairs(lines, depth):
    return [
        (device(line, place, core, depth), device((line - 1 + 2 * core) % lines, place, core, depth))
        for line in range(lines)
        for place in range(2 * depth)
        for core in range(2)
        if place % depth != (depth - 1 if core == 0 else 0)
    ]


def split(value):
    high = value.astype(jnp.bfloat16)
    return high, (value - high.astype(jnp.float32)).astype(jnp.bfloat16)


def step_kernel(depth, slots, step, rows, targets, pairs, fresh, pieces, info, *refs):
    held = []
    for count in pieces:
        held.append(refs[:count])
        refs = refs[count:]
    factors, refs = refs[: len(targets)], refs[len(targets) :]
    if not fresh:
        refs = refs[len(targets) :]
    sums, refs = refs[: len(targets)], refs[len(targets) :]
    row_buf, factor_buf, sum_buf, row_sem, factor_sem, sum_sem = refs
    width = max(pieces)

    place, core = info[0], info[1]
    half, low = place // depth, place % depth
    there = (place + 2 * depth - step + 2 * step * core) % (2 * depth)
    origin, cls = there // depth, there % depth
    line_rows = 4 * depth

    def column(row, slot):
        return info[2 + row * slots + slot]

    def held_row(which):
        q = core + which * (1 - 2 * core)
        line = 1 + jnp.where(origin == q, half - origin, 0)
        return line_rows * line + 2 * depth * origin + depth * q + cls

    def target_row(which):
        q = core + (which == 1) * (1 - 2 * core)
        line = 1 + (which == 2) * (1 - 2 * core)
        return line_rows * line + 2 * depth * half + depth * q + low

    def find(k, i):
        more = jnp.minimum(cls + depth, slots - 1)
        first = column(i, cls) == k
        second = jnp.logical_and(cls + depth < slots, column(i, more) == k)
        return jnp.logical_or(first, second), jnp.where(first, cls, more)

    k_of = [held_row(r) for r in rows]
    i_of = [target_row(t) for t in targets]
    found = [find(k_of[r], i_of[t]) for r, t in pairs]

    def any_of(where):
        return functools.reduce(jnp.logical_or, [f[0] for f, p in zip(found, pairs) if where(p)])

    row_used = [any_of(lambda p, r=r: p[0] == r) for r in range(len(rows))]
    sum_used = [any_of(lambda p, t=t: p[1] == t) for t in range(len(targets))]

    def row_copies(r):
        out, at = [], 0
        for n, piece in enumerate(held[r]):
            here = row_buf.at[r, pl.ds(at, piece.shape[0])]
            out.append(pltpu.make_async_copy(piece, here, row_sem.at[r * width + n]))
            at += piece.shape[0]
        return out

    def factor_copy(n):
        t = pairs[n][1]
        return pltpu.make_async_copy(
            factors[t].at[found[n][1]], factor_buf.at[n], factor_sem.at[n]
        )

    def sum_load(t):
        return pltpu.make_async_copy(sums[t], sum_buf.at[t], sum_sem.at[t])

    def sum_store(t):
        return pltpu.make_async_copy(sum_buf.at[t], sums[t], sum_sem.at[t])

    for phase in ("start", "wait"):
        for r in range(len(rows)):
            for copy in row_copies(r):
                pl.when(row_used[r])(getattr(copy, phase))
        for n in range(len(pairs)):
            pl.when(found[n][0])(getattr(factor_copy(n), phase))
        if not fresh:
            for t in range(len(targets)):
                pl.when(sum_used[t])(getattr(sum_load(t), phase))
        elif phase == "start":
            for t in range(len(targets)):
                sum_buf[t] = jnp.zeros(sum_buf.shape[1:], jnp.float32)

    def select(options, n):
        out = options[0]
        for m in range(1, len(options)):
            out = jnp.where(n == m, options[m], out)
        return out

    def product(n, carry):
        r = select([p[0] for p in pairs], n)
        t = select([p[1] for p in pairs], n)
        k, i = select(k_of, r), select(i_of, t)

        @pl.when(find(k, i)[0])
        def _():
            a_high, a_low = split(factor_buf[n])
            for pair in range(0, slots, 2):
                blocks = []
                for o in (pair, pair + 1):
                    goal = column(i, o)
                    match, where = column(k, o) == goal, o
                    twin = o + depth if o + depth < slots else o - depth
                    if twin >= 0:
                        second = column(k, twin) == goal
                        match, where = jnp.logical_or(match, second), jnp.where(second, twin, o)
                    block = row_buf[r, where]
                    blocks.append(jnp.where(match, block, jnp.zeros_like(block)))
                b_high, b_low = split(jnp.concatenate(blocks, axis=1))
                dot = functools.partial(jnp.dot, preferred_element_type=jnp.float32)
                part = dot(a_high, b_high) + (dot(a_high, b_low) + dot(a_low, b_high))
                edge = part.shape[0]
                sum_buf[t, pair] += part[:, :edge]
                sum_buf[t, pair + 1] += part[:, edge:]

        return carry

    lax.fori_loop(0, len(pairs), product, 0)

    for phase in ("start", "wait"):
        for t in range(len(targets)):
            if fresh:
                getattr(sum_store(t), phase)()
            else:
                pl.when(sum_used[t])(getattr(sum_store(t), phase))


def step_call(depth, step, rows, targets, pairs, info, held, factors, sums=None):
    slots, edge = factors[0].shape[:2]
    fresh = sums is None
    shape = jax.ShapeDtypeStruct(factors[0].shape, jnp.float32)
    hbm = pl.BlockSpec(memory_space=pl.ANY)
    pieces = tuple(len(row) for row in held)
    operands = [info, *sum(held, []), *factors] + ([] if fresh else list(sums))
    first = 1 + sum(pieces) + len(factors)
    return list(
        pl.pallas_call(
            functools.partial(step_kernel, depth, slots, step, rows, targets, pairs, fresh, pieces),
            out_shape=[shape] * len(targets),
            in_specs=[pl.BlockSpec(memory_space=pltpu.SMEM)] + [hbm] * (len(operands) - 1),
            out_specs=[hbm] * len(targets),
            input_output_aliases={} if fresh else {first + t: t for t in range(len(targets))},
            scratch_shapes=[
                pltpu.VMEM((len(rows), *shape.shape), jnp.float32),
                pltpu.VMEM((len(pairs), edge, edge), jnp.float32),
                pltpu.VMEM((len(targets), *shape.shape), jnp.float32),
                pltpu.SemaphoreType.DMA((len(rows) * max(pieces),)),
                pltpu.SemaphoreType.DMA((len(pairs),)),
                pltpu.SemaphoreType.DMA((len(targets),)),
            ],
            compiler_params=pltpu.CompilerParams(vmem_limit_bytes=24 << 20),
            cost_estimate=pl.CostEstimate(
                flops=200_000_000, bytes_accessed=8_000_000, transcendentals=0
            ),
            name="products",
        )(*operands)
    )


def body(blocks, columns):
    depth = lax.axis_size("depth")
    lines = lax.axis_size("row")
    block_rows, slots = columns.shape
    line_rows = 4 * depth
    ring, every = ("col", "depth"), ("row", "col", "depth")
    col = lax.axis_index("col")
    place = (col // 2) * depth + lax.axis_index("depth")
    base = (lax.axis_index("row") - 1) * line_rows + block_rows
    near = jnp.take(columns, (base + jnp.arange(3 * line_rows)) % block_rows, axis=0)
    near = (near - base + 2 * block_rows) % block_rows
    info = jnp.concatenate(
        [jnp.stack([place, col % 2]).astype(jnp.int32), near.reshape(-1)]
    )

    def hop(held, step, which):
        pairs = hop_pairs(lines, depth, step, which)
        return [lax.ppermute(piece, every, pairs) for piece in held[which]]

    def flip(value):
        return lax.ppermute(value, ring, flip_pairs(depth))

    own = blocks[0]
    other, info = lax.optimization_barrier((flip(own), info))
    away = line_pairs(lines, depth)
    ghost = lax.ppermute(own, every, away)
    factors = [own, other, ghost]
    sums = step_call(
        depth, 0, (0, 1), (0,), ((0, 0), (1, 0)), info, [[own], [other]], factors[:1]
    )
    sums += [jnp.zeros_like(own) for _ in range(2)]
    held = [
        [value[a:b] for a, b in zip((0, *cuts), (*cuts, slots))]
        for value, cuts in zip((own, other), CUTS)
    ]
    held = [hop(held, 1, which) for which in range(2)]
    for step in range(1, depth - 1):
        held[0][0], sums = lax.optimization_barrier((held[0][0], sums))
        going = [held[0], held[1] if step < depth - 2 else [jnp.concatenate(held[1])]]
        after = [hop(going, step + 1, which) for which in range(2)]
        pairs = ((0, 0), (0, 1), (0, 2), (1, 0), (1, 1))
        sums = step_call(depth, step, (0, 1), (0, 1, 2), pairs, info, held, factors, sums)
        held = after
    last = depth - 1
    held[0][0], sums = lax.optimization_barrier((held[0][0], sums))
    far = [
        p for p in hop_pairs(lines, depth, depth, 0, across=True) if p[1] % depth < slots - depth
    ]
    far = [lax.ppermute(jnp.concatenate(held[0]), every, far)]
    (foreign,) = step_call(
        depth, last, (0,), (2,), ((0, 0),), info, held[:1], factors[2:], sums[2:]
    )
    foreign = lax.ppermute(foreign, every, [(b, a) for a, b in away])
    mine, other = step_call(
        depth, last, (0, 1), (0, 1), ((0, 0), (0, 1), (1, 0), (1, 1)), info, held, factors[:2], sums[:2]
    )
    other = flip(other)
    (mine,) = step_call(depth, depth, (1,), (0,), ((0, 0),), info, [far], factors[:1], [mine])
    return (mine + other + foreign)[None]


def solution(mesh):
    placed = (P(("row", "col", "depth"), None, None, None), P())
    return jax.shard_map(
        body,
        mesh=mesh,
        in_specs=placed,
        out_specs=P(("row", "col", "depth"), None, None, None),
        check_vma=False,
    )
```

```python
import functools

import jax
import jax.numpy as jnp
from jax import lax
from jax.experimental import pallas as pl
from jax.experimental.pallas import tpu as pltpu
from jax.sharding import PartitionSpec as P


CUTS = ((5,), (5,))


def device(line, place, core, depth):
    return ((line * 2 + place // depth) * 2 + core) * depth + place % depth


def hop_pairs(lines, depth, step, which, across=False):
    pairs = []
    for line in range(lines):
        for place in range(2 * depth):
            for core in range(2):
                way = 1 - 2 * core
                origin = (place - way * (step - 1)) % (2 * depth)
                to = (place + way) % (2 * depth)
                crosses = place // depth - to // depth if origin // depth == core ^ which else 0
                pairs.append(
                    (
                        device(line, place, core, depth),
                        device((line + crosses) % lines, to, core ^ across, depth),
                    )
                )
    return pairs


def flip_pairs(depth):
    return [(n, n ^ depth) for n in range(4 * depth)]


def line_pairs(lines, depth):
    return [
        (device(line, place, core, depth), device((line - 1 + 2 * core) % lines, place, core, depth))
        for line in range(lines)
        for place in range(2 * depth)
        for core in range(2)
        if place % depth != (depth - 1 if core == 0 else 0)
    ]


def split(value):
    high = value.astype(jnp.bfloat16)
    return high, (value - high.astype(jnp.float32)).astype(jnp.bfloat16)


def step_kernel(depth, slots, step, rows, targets, pairs, fresh, pieces, info, *refs):
    held = []
    for count in pieces:
        held.append(refs[:count])
        refs = refs[count:]
    factors, refs = refs[: len(targets)], refs[len(targets) :]
    if not fresh:
        refs = refs[len(targets) :]
    sums, refs = refs[: len(targets)], refs[len(targets) :]
    row_buf, factor_buf, sum_buf, row_sem, factor_sem, sum_sem = refs
    width = max(pieces)

    place, core = info[0], info[1]
    half, low = place // depth, place % depth
    there = (place + 2 * depth - step + 2 * step * core) % (2 * depth)
    origin, cls = there // depth, there % depth
    line_rows = 4 * depth

    def column(row, slot):
        return info[2 + row * slots + slot]

    def held_row(which):
        q = core + which * (1 - 2 * core)
        line = 1 + jnp.where(origin == q, half - origin, 0)
        return line_rows * line + 2 * depth * origin + depth * q + cls

    def target_row(which):
        q = core + (which == 1) * (1 - 2 * core)
        line = 1 + (which == 2) * (1 - 2 * core)
        return line_rows * line + 2 * depth * half + depth * q + low

    def find(k, i):
        more = jnp.minimum(cls + depth, slots - 1)
        first = column(i, cls) == k
        second = jnp.logical_and(cls + depth < slots, column(i, more) == k)
        return jnp.logical_or(first, second), jnp.where(first, cls, more)

    k_of = [held_row(r) for r in rows]
    i_of = [target_row(t) for t in targets]
    found = [find(k_of[r], i_of[t]) for r, t in pairs]

    def any_of(where):
        return functools.reduce(jnp.logical_or, [f[0] for f, p in zip(found, pairs) if where(p)])

    row_used = [any_of(lambda p, r=r: p[0] == r) for r in range(len(rows))]
    sum_used = [any_of(lambda p, t=t: p[1] == t) for t in range(len(targets))]

    def row_copies(r):
        out, at = [], 0
        for n, piece in enumerate(held[r]):
            here = row_buf.at[r, pl.ds(at, piece.shape[0])]
            out.append(pltpu.make_async_copy(piece, here, row_sem.at[r * width + n]))
            at += piece.shape[0]
        return out

    def factor_copy(n):
        t = pairs[n][1]
        return pltpu.make_async_copy(
            factors[t].at[found[n][1]], factor_buf.at[n], factor_sem.at[n]
        )

    def sum_load(t):
        return pltpu.make_async_copy(sums[t], sum_buf.at[t], sum_sem.at[t])

    def sum_store(t):
        return pltpu.make_async_copy(sum_buf.at[t], sums[t], sum_sem.at[t])

    for phase in ("start", "wait"):
        for r in range(len(rows)):
            for copy in row_copies(r):
                pl.when(row_used[r])(getattr(copy, phase))
        for n in range(len(pairs)):
            pl.when(found[n][0])(getattr(factor_copy(n), phase))
        if not fresh:
            for t in range(len(targets)):
                pl.when(sum_used[t])(getattr(sum_load(t), phase))
        elif phase == "start":
            for t in range(len(targets)):
                sum_buf[t] = jnp.zeros(sum_buf.shape[1:], jnp.float32)

    def select(options, n):
        out = options[0]
        for m in range(1, len(options)):
            out = jnp.where(n == m, options[m], out)
        return out

    def product(n, carry):
        r = select([p[0] for p in pairs], n)
        t = select([p[1] for p in pairs], n)
        k, i = select(k_of, r), select(i_of, t)

        @pl.when(find(k, i)[0])
        def _():
            a_high, a_low = split(factor_buf[n])
            for pair in range(0, slots, 2):
                blocks = []
                for o in (pair, pair + 1):
                    goal = column(i, o)
                    match, where = column(k, o) == goal, o
                    twin = o + depth if o + depth < slots else o - depth
                    if twin >= 0:
                        second = column(k, twin) == goal
                        match, where = jnp.logical_or(match, second), jnp.where(second, twin, o)
                    block = row_buf[r, where]
                    blocks.append(jnp.where(match, block, jnp.zeros_like(block)))
                b_high, b_low = split(jnp.concatenate(blocks, axis=1))
                dot = functools.partial(jnp.dot, preferred_element_type=jnp.float32)
                part = dot(a_high, b_high) + (dot(a_high, b_low) + dot(a_low, b_high))
                edge = part.shape[0]
                sum_buf[t, pair] += part[:, :edge]
                sum_buf[t, pair + 1] += part[:, edge:]

        return carry

    lax.fori_loop(0, len(pairs), product, 0)

    for phase in ("start", "wait"):
        for t in range(len(targets)):
            if fresh:
                getattr(sum_store(t), phase)()
            else:
                pl.when(sum_used[t])(getattr(sum_store(t), phase))


def step_call(depth, step, rows, targets, pairs, info, held, factors, sums=None):
    slots, edge = factors[0].shape[:2]
    fresh = sums is None
    shape = jax.ShapeDtypeStruct(factors[0].shape, jnp.float32)
    hbm = pl.BlockSpec(memory_space=pl.ANY)
    pieces = tuple(len(row) for row in held)
    operands = [info, *sum(held, []), *factors] + ([] if fresh else list(sums))
    first = 1 + sum(pieces) + len(factors)
    return list(
        pl.pallas_call(
            functools.partial(step_kernel, depth, slots, step, rows, targets, pairs, fresh, pieces),
            out_shape=[shape] * len(targets),
            in_specs=[pl.BlockSpec(memory_space=pltpu.SMEM)] + [hbm] * (len(operands) - 1),
            out_specs=[hbm] * len(targets),
            input_output_aliases={} if fresh else {first + t: t for t in range(len(targets))},
            scratch_shapes=[
                pltpu.VMEM((len(rows), *shape.shape), jnp.float32),
                pltpu.VMEM((len(pairs), edge, edge), jnp.float32),
                pltpu.VMEM((len(targets), *shape.shape), jnp.float32),
                pltpu.SemaphoreType.DMA((len(rows) * max(pieces),)),
                pltpu.SemaphoreType.DMA((len(pairs),)),
                pltpu.SemaphoreType.DMA((len(targets),)),
            ],
            compiler_params=pltpu.CompilerParams(vmem_limit_bytes=24 << 20),
            cost_estimate=pl.CostEstimate(
                flops=200_000_000, bytes_accessed=8_000_000, transcendentals=0
            ),
            name="products",
        )(*operands)
    )


def body(blocks, columns):
    depth = lax.axis_size("depth")
    lines = lax.axis_size("row")
    block_rows, slots = columns.shape
    line_rows = 4 * depth
    ring, every = ("col", "depth"), ("row", "col", "depth")
    col = lax.axis_index("col")
    place = (col // 2) * depth + lax.axis_index("depth")
    base = (lax.axis_index("row") - 1) * line_rows + block_rows
    near = jnp.take(columns, (base + jnp.arange(3 * line_rows)) % block_rows, axis=0)
    near = (near - base + 2 * block_rows) % block_rows
    info = jnp.concatenate(
        [jnp.stack([place, col % 2]).astype(jnp.int32), near.reshape(-1)]
    )

    def hop(held, step, which):
        pairs = hop_pairs(lines, depth, step, which)
        return [lax.ppermute(piece, every, pairs) for piece in held[which]]

    def flip(value):
        return lax.ppermute(value, ring, flip_pairs(depth))

    own = blocks[0]
    other = flip(own)
    away = line_pairs(lines, depth)
    factors = [own]
    sums = step_call(
        depth, 0, (0, 1), (0,), ((0, 0), (1, 0)), info, [[own], [other]], factors[:1]
    )
    sums += [jnp.zeros_like(own) for _ in range(2)]
    held = [
        [value[a:b] for a, b in zip((0, *cuts), (*cuts, slots))]
        for value, cuts in zip((own, other), CUTS)
    ]
    held = [hop(held, 1, which) for which in range(2)]
    later, held[0][0] = lax.optimization_barrier((own, held[0][0]))
    factors = [own, other, lax.ppermute(later, every, away)]
    for step in range(1, depth - 1):
        held[0][0], sums = lax.optimization_barrier((held[0][0], sums))
        going = [held[0], held[1] if step < depth - 2 else [jnp.concatenate(held[1])]]
        after = [hop(going, step + 1, which) for which in range(2)]
        pairs = ((0, 0), (0, 1), (0, 2), (1, 0), (1, 1))
        sums = step_call(depth, step, (0, 1), (0, 1, 2), pairs, info, held, factors, sums)
        held = after
    last = depth - 1
    held[0][0], sums = lax.optimization_barrier((held[0][0], sums))
    far = [
        p for p in hop_pairs(lines, depth, depth, 0, across=True) if p[1] % depth < slots - depth
    ]
    far = [lax.ppermute(jnp.concatenate(held[0]), every, far)]
    (foreign,) = step_call(
        depth, last, (0,), (2,), ((0, 0),), info, held[:1], factors[2:], sums[2:]
    )
    foreign = lax.ppermute(foreign, every, [(b, a) for a, b in away])
    mine, other = step_call(
        depth, last, (0, 1), (0, 1), ((0, 0), (0, 1), (1, 0), (1, 1)), info, held, factors[:2], sums[:2]
    )
    other = flip(other)
    (mine,) = step_call(depth, depth, (1,), (0,), ((0, 0),), info, [far], factors[:1], [mine])
    return (mine + other + foreign)[None]


def solution(mesh):
    placed = (P(("row", "col", "depth"), None, None, None), P())
    return jax.shard_map(
        body,
        mesh=mesh,
        in_specs=placed,
        out_specs=P(("row", "col", "depth"), None, None, None),
        check_vma=False,
    )
```

```python
import functools

import jax
import jax.numpy as jnp
from jax import lax
from jax.experimental import pallas as pl
from jax.experimental.pallas import tpu as pltpu
from jax.sharding import PartitionSpec as P


CUTS = ((5,), (5,))


def device(line, place, core, depth):
    return ((line * 2 + place // depth) * 2 + core) * depth + place % depth


def hop_pairs(lines, depth, step, which, across=False):
    pairs = []
    for line in range(lines):
        for place in range(2 * depth):
            for core in range(2):
                way = 1 - 2 * core
                origin = (place - way * (step - 1)) % (2 * depth)
                to = (place + way) % (2 * depth)
                crosses = place // depth - to // depth if origin // depth == core ^ which else 0
                pairs.append(
                    (
                        device(line, place, core, depth),
                        device((line + crosses) % lines, to, core ^ across, depth),
                    )
                )
    return pairs


def flip_pairs(depth):
    return [(n, n ^ depth) for n in range(4 * depth)]


def line_pairs(lines, depth):
    return [
        (device(line, place, core, depth), device((line - 1 + 2 * core) % lines, place, core, depth))
        for line in range(lines)
        for place in range(2 * depth)
        for core in range(2)
        if place % depth != (depth - 1 if core == 0 else 0)
    ]


def split(value):
    high = value.astype(jnp.bfloat16)
    return high, (value - high.astype(jnp.float32)).astype(jnp.bfloat16)


def step_kernel(depth, slots, step, rows, targets, pairs, fresh, pieces, info, *refs):
    held = []
    for count in pieces:
        held.append(refs[:count])
        refs = refs[count:]
    factors, refs = refs[: len(targets)], refs[len(targets) :]
    if not fresh:
        refs = refs[len(targets) :]
    sums, refs = refs[: len(targets)], refs[len(targets) :]
    row_buf, factor_buf, sum_buf, row_sem, factor_sem, sum_sem = refs
    width = max(pieces)

    place, core = info[0], info[1]
    half, low = place // depth, place % depth
    there = (place + 2 * depth - step + 2 * step * core) % (2 * depth)
    origin, cls = there // depth, there % depth
    line_rows = 4 * depth

    def column(row, slot):
        return info[2 + row * slots + slot]

    def held_row(which):
        q = core + which * (1 - 2 * core)
        line = 1 + jnp.where(origin == q, half - origin, 0)
        return line_rows * line + 2 * depth * origin + depth * q + cls

    def target_row(which):
        q = core + (which == 1) * (1 - 2 * core)
        line = 1 + (which == 2) * (1 - 2 * core)
        return line_rows * line + 2 * depth * half + depth * q + low

    def find(k, i):
        more = jnp.minimum(cls + depth, slots - 1)
        first = column(i, cls) == k
        second = jnp.logical_and(cls + depth < slots, column(i, more) == k)
        return jnp.logical_or(first, second), jnp.where(first, cls, more)

    k_of = [held_row(r) for r in rows]
    i_of = [target_row(t) for t in targets]
    found = [find(k_of[r], i_of[t]) for r, t in pairs]

    def any_of(where):
        return functools.reduce(jnp.logical_or, [f[0] for f, p in zip(found, pairs) if where(p)])

    row_used = [any_of(lambda p, r=r: p[0] == r) for r in range(len(rows))]
    sum_used = [any_of(lambda p, t=t: p[1] == t) for t in range(len(targets))]

    def row_copies(r):
        out, at = [], 0
        for n, piece in enumerate(held[r]):
            here = row_buf.at[r, pl.ds(at, piece.shape[0])]
            out.append(pltpu.make_async_copy(piece, here, row_sem.at[r * width + n]))
            at += piece.shape[0]
        return out

    def factor_copy(n):
        t = pairs[n][1]
        return pltpu.make_async_copy(
            factors[t].at[found[n][1]], factor_buf.at[n], factor_sem.at[n]
        )

    def sum_load(t):
        return pltpu.make_async_copy(sums[t], sum_buf.at[t], sum_sem.at[t])

    def sum_store(t):
        return pltpu.make_async_copy(sum_buf.at[t], sums[t], sum_sem.at[t])

    for phase in ("start", "wait"):
        for r in range(len(rows)):
            for copy in row_copies(r):
                pl.when(row_used[r])(getattr(copy, phase))
        for n in range(len(pairs)):
            pl.when(found[n][0])(getattr(factor_copy(n), phase))
        if not fresh:
            for t in range(len(targets)):
                pl.when(sum_used[t])(getattr(sum_load(t), phase))
        elif phase == "start":
            for t in range(len(targets)):
                sum_buf[t] = jnp.zeros(sum_buf.shape[1:], jnp.float32)

    def select(options, n):
        out = options[0]
        for m in range(1, len(options)):
            out = jnp.where(n == m, options[m], out)
        return out

    def product(n, carry):
        r = select([p[0] for p in pairs], n)
        t = select([p[1] for p in pairs], n)
        k, i = select(k_of, r), select(i_of, t)

        @pl.when(find(k, i)[0])
        def _():
            a_high, a_low = split(factor_buf[n])
            for pair in range(0, slots, 2):
                blocks = []
                for o in (pair, pair + 1):
                    goal = column(i, o)
                    match, where = column(k, o) == goal, o
                    twin = o + depth if o + depth < slots else o - depth
                    if twin >= 0:
                        second = column(k, twin) == goal
                        match, where = jnp.logical_or(match, second), jnp.where(second, twin, o)
                    block = row_buf[r, where]
                    blocks.append(jnp.where(match, block, jnp.zeros_like(block)))
                b_high, b_low = split(jnp.concatenate(blocks, axis=1))
                dot = functools.partial(jnp.dot, preferred_element_type=jnp.float32)
                part = dot(a_high, b_high) + (dot(a_high, b_low) + dot(a_low, b_high))
                edge = part.shape[0]
                sum_buf[t, pair] += part[:, :edge]
                sum_buf[t, pair + 1] += part[:, edge:]

        return carry

    lax.fori_loop(0, len(pairs), product, 0)

    for phase in ("start", "wait"):
        for t in range(len(targets)):
            if fresh:
                getattr(sum_store(t), phase)()
            else:
                pl.when(sum_used[t])(getattr(sum_store(t), phase))


def step_call(depth, step, rows, targets, pairs, info, held, factors, sums=None):
    slots, edge = factors[0].shape[:2]
    fresh = sums is None
    shape = jax.ShapeDtypeStruct(factors[0].shape, jnp.float32)
    hbm = pl.BlockSpec(memory_space=pl.ANY)
    pieces = tuple(len(row) for row in held)
    operands = [info, *sum(held, []), *factors] + ([] if fresh else list(sums))
    first = 1 + sum(pieces) + len(factors)
    return list(
        pl.pallas_call(
            functools.partial(step_kernel, depth, slots, step, rows, targets, pairs, fresh, pieces),
            out_shape=[shape] * len(targets),
            in_specs=[pl.BlockSpec(memory_space=pltpu.SMEM)] + [hbm] * (len(operands) - 1),
            out_specs=[hbm] * len(targets),
            input_output_aliases={} if fresh else {first + t: t for t in range(len(targets))},
            scratch_shapes=[
                pltpu.VMEM((len(rows), *shape.shape), jnp.float32),
                pltpu.VMEM((len(pairs), edge, edge), jnp.float32),
                pltpu.VMEM((len(targets), *shape.shape), jnp.float32),
                pltpu.SemaphoreType.DMA((len(rows) * max(pieces),)),
                pltpu.SemaphoreType.DMA((len(pairs),)),
                pltpu.SemaphoreType.DMA((len(targets),)),
            ],
            compiler_params=pltpu.CompilerParams(vmem_limit_bytes=24 << 20),
            cost_estimate=pl.CostEstimate(
                flops=200_000_000, bytes_accessed=8_000_000, transcendentals=0
            ),
            name="products",
        )(*operands)
    )


def body(blocks, columns):
    depth = lax.axis_size("depth")
    lines = lax.axis_size("row")
    block_rows, slots = columns.shape
    line_rows = 4 * depth
    ring, every = ("col", "depth"), ("row", "col", "depth")
    col = lax.axis_index("col")
    place = (col // 2) * depth + lax.axis_index("depth")
    base = (lax.axis_index("row") - 1) * line_rows + block_rows
    near = jnp.take(columns, (base + jnp.arange(3 * line_rows)) % block_rows, axis=0)
    near = (near - base + 2 * block_rows) % block_rows
    info = jnp.concatenate(
        [jnp.stack([place, col % 2]).astype(jnp.int32), near.reshape(-1)]
    )

    def hop(held, step, which):
        pairs = hop_pairs(lines, depth, step, which)
        return [lax.ppermute(piece, every, pairs) for piece in held[which]]

    def flip(value):
        return lax.ppermute(value, ring, flip_pairs(depth))

    own = blocks[0]
    other = flip(own)
    away = line_pairs(lines, depth)
    later, info = lax.optimization_barrier((own, info))
    ghost = lax.ppermute(later, every, away)
    factors = [own, other, ghost]
    sums = step_call(
        depth, 0, (0, 1), (0,), ((0, 0), (1, 0)), info, [[own], [other]], factors[:1]
    )
    sums += [jnp.zeros_like(own) for _ in range(2)]
    held = [
        [value[a:b] for a, b in zip((0, *cuts), (*cuts, slots))]
        for value, cuts in zip((own, other), CUTS)
    ]
    held = [hop(held, 1, which) for which in range(2)]
    for step in range(1, depth - 1):
        held[0][0], sums = lax.optimization_barrier((held[0][0], sums))
        going = [held[0], held[1] if step < depth - 2 else [jnp.concatenate(held[1])]]
        after = [hop(going, step + 1, which) for which in range(2)]
        pairs = ((0, 0), (0, 1), (0, 2), (1, 0), (1, 1))
        sums = step_call(depth, step, (0, 1), (0, 1, 2), pairs, info, held, factors, sums)
        held = after
    last = depth - 1
    held[0][0], sums = lax.optimization_barrier((held[0][0], sums))
    far = [
        p for p in hop_pairs(lines, depth, depth, 0, across=True) if p[1] % depth < slots - depth
    ]
    far = [lax.ppermute(jnp.concatenate(held[0]), every, far)]
    (foreign,) = step_call(
        depth, last, (0,), (2,), ((0, 0),), info, held[:1], factors[2:], sums[2:]
    )
    foreign = lax.ppermute(foreign, every, [(b, a) for a, b in away])
    mine, other = step_call(
        depth, last, (0, 1), (0, 1), ((0, 0), (0, 1), (1, 0), (1, 1)), info, held, factors[:2], sums[:2]
    )
    other = flip(other)
    (mine,) = step_call(depth, depth, (1,), (0,), ((0, 0),), info, [far], factors[:1], [mine])
    return (mine + other + foreign)[None]


def solution(mesh):
    placed = (P(("row", "col", "depth"), None, None, None), P())
    return jax.shard_map(
        body,
        mesh=mesh,
        in_specs=placed,
        out_specs=P(("row", "col", "depth"), None, None, None),
        check_vma=False,
    )
```
